256 devices in a mesh: rows: 64 (over y, z, core), feat: 4 (over x).
Axes of the slice: x: 4, y: 4, z: 8, core: 2. Of those that a mesh axis runs over, the one named last changes fastest.
Arguments:
- embeddings: bfloat16 [131072, 1024], P('rows', 'feat'), may hold values from -8 to 8
- parent_ids: int32 [131072, 1], P('rows'), may hold values from 0 to 63; in each aligned block of 2048 rows (0 to 2047, 2048 to 4095, ...) at most 64 rows name the same one
- child_assignment: int32 [131072], P('rows'), may hold values from 0 to 63
Outputs:
- centroids: bfloat16 [4096, 1024], P('rows', 'feat')
- row_fit: float32 [131072], P('rows')
The draws below stay inside these ranges and needn't reach their ends.
Inputs may be any that keep to these rules, and one draw needn't show every extreme that they name: `parent_ids`: in the rows of one index of rows, at most 64 rows name any one parent, a bound that some block reaches.
All inputs are finite; a program needn't handle non-finite values.
Results may differ from the reference program's by a relative error of at most 0.011.
Values may be sent and summed in bfloat16 or wider, within the bound.
No kernel may reach another device: no remote copies, remote signals or barrier semaphores. Data moves between devices by JAX's collectives and lax.ppermute only.
A program may use at most 64 MiB of HBM per device.

```python
import math
import jax
import jax.numpy as jnp
import numpy as np
from jax import lax

D = 1024
K = 64
ROW_DEV = 2048
PARENTS = 64
CAP = 64
ROWS = 131072


def draw_embeddings(key, part):
    key = jax.random.fold_in(key, 11)
    key_cols, key_rows, key_base = jax.random.split(key, 3)
    column_scale = 0.3 * jnp.exp(jax.random.uniform(key_cols, (1, D), jnp.float32, 0.0, jnp.log(10.0)))
    row_scale = jnp.exp(jax.random.uniform(key_rows, (ROWS, 1), jnp.float32, jnp.log(0.5), jnp.log(2.0)))
    base = jax.random.normal(key_base, (ROWS, D), jnp.float32)
    values = base * column_scale * row_scale
    return jnp.clip(values, -8.0, 8.0).astype(jnp.bfloat16)


def set_ends(result, rng, least, top_value):
    longest = result.shape.index(max(result.shape))
    spots = []
    for shift in (0, 1):
        where = [jax.random.randint(jax.random.fold_in(rng, axis), (), 0, length) for axis, length in enumerate(result.shape)]
        where[longest] = (where[longest] + shift) % result.shape[longest]
        spots.append(tuple(where))
    return result.at[spots[0]].set(least).at[spots[1]].set(top_value)


def deal_out(key, own, number, rows, amount, top, most, slope):
    order = jax.random.permutation(key, amount)
    crowded, usual = portions_of(amount, rows * top, most, slope, True), portions_of(amount, rows * top, most, slope, False)
    places = jnp.arange(amount)

    def named(tallies, turn):
        used = int((tallies > 0).sum())
        fixed = max(1, used // 4)
        shifted = fixed + (places - fixed + turn * (used - fixed)) % max(1, amount - fixed)
        return jnp.zeros((amount,), jnp.int32).at[order[jnp.where(places < fixed, places, shifted)]].set(jnp.asarray(tallies, jnp.int32))

    tallies = jnp.where(number % 4 == 0, named(crowded, number // 4), named(usual, number - number // 4 - 1))
    mixed = jax.random.permutation(jax.random.fold_in(own, 3), amount)
    donor, receiver = mixed[0:amount // 2 * 2:2], mixed[1:amount // 2 * 2:2]
    margin = jnp.minimum(tallies[donor] - 1, most - tallies[receiver]) // 2
    margin = jnp.where((donor == order[0]) | (receiver == order[0]) | (tallies[receiver] == 0), 0, jnp.maximum(margin, 0))
    shifted = jax.random.randint(jax.random.fold_in(own, 4), (amount // 2,), 0, 1 << 20) % (margin + 1)
    tallies = tallies.at[donor].add(-shifted).at[receiver].add(shifted)
    items = jnp.searchsorted(jnp.cumsum(tallies), jnp.arange(rows * top), side="right").astype(jnp.int32)
    table = items.reshape(top, rows).T
    table = table[jax.random.permutation(jax.random.fold_in(own, 1), rows)]
    turn = jax.random.randint(jax.random.fold_in(own, 2), (rows, 1), 0, top)
    return jnp.take_along_axis(table, (jnp.arange(top)[None, :] + turn) % top, axis=1)


def portions_of(amount, total, limit, lean, full):
    portions = [(1 << 20) // math.isqrt(grade ** lean) + 1 for grade in range(1, amount + 1)]
    largest = limit if full else min(limit, max(-(-total // amount), total * portions[0] // sum(portions)))
    least = 1 if total - largest >= amount - 1 else 0
    counts, spare = [largest] + [least] * (amount - 1), total - largest - least * (amount - 1)
    while spare > 0:
        free = [i for i in range(1, amount) if counts[i] < largest] or [i for i in range(1, amount) if counts[i] < limit]
        whole, remaining = sum([portions[i] for i in free]), spare
        for i in free:
            extra = min(limit - counts[i], max(1, remaining * portions[i] // whole), spare)
            counts[i] = counts[i] + extra
            spare = spare - extra
    return np.array(counts)


def setup_inputs(seed: int = 0) -> dict:
    arg_keys = jax.random.split(jax.random.key(seed), 4)
    embeddings = draw_embeddings(jax.random.fold_in(arg_keys[3], 71), 0)
    parent_ids_keys = jax.random.split(jax.random.fold_in(arg_keys[1], 1), ROWS // ROW_DEV)
    parent_ids_turns = jax.random.permutation(jax.random.fold_in(arg_keys[1], 3), ROWS // ROW_DEV)
    parent_ids = jax.vmap(lambda own, number: deal_out(jax.random.fold_in(arg_keys[1], 2), own, number, ROW_DEV, PARENTS, 1, CAP, 2))(parent_ids_keys, parent_ids_turns).reshape((ROWS, 1))
    child_assignment = set_ends(jax.random.randint(arg_keys[2], (ROWS,), 0, K), jax.random.fold_in(arg_keys[2], 1), 0, K - 1).astype(jnp.int32)
    return {"embeddings": embeddings, "parent_ids": parent_ids, "child_assignment": child_assignment}


epsilon = 1e-06

def reference(embeddings, parent_ids, child_assignment):
    parent = parent_ids[:, 0]
    cluster_group_index = (parent * K + child_assignment).astype(jnp.int32)
    totals = jax.ops.segment_sum(embeddings.astype(jnp.float32), cluster_group_index, num_segments=PARENTS * K)
    squares = lax.optimization_barrier(jnp.mean(totals * totals, axis=1, keepdims=True))
    centroids = (totals * lax.rsqrt(squares + epsilon)).astype(jnp.bfloat16)
    row_block = min(512, ROWS)
    blocks = ROWS // row_block

    def score_block(turn_index):
        first_row = (turn_index * row_block).astype(jnp.int32)
        row_portion = lax.dynamic_slice_in_dim(embeddings, first_row, row_block, 0).astype(jnp.float32)
        parent_part = lax.dynamic_slice_in_dim(parent, first_row, row_block, 0)
        indices = (parent_part[:, None] * K + jnp.arange(K, dtype=jnp.int32)[None, :]).astype(jnp.int32)
        selected_child = centroids[indices].astype(jnp.float32)
        distance_scores = jnp.einsum('wc,wtc->wt', row_portion, selected_child, precision=lax.Precision.HIGHEST)
        return lax.optimization_barrier(jnp.max(distance_scores, axis=1)) / (0.25 * D)
    row_fit = lax.map(score_block, jnp.arange(blocks, dtype=jnp.int32)).reshape(ROWS)
    return (centroids, row_fit)
```

```python
import functools

import jax
import jax.numpy as jnp
from jax import lax
from jax.experimental import pallas as pl
from jax.experimental.pallas import tpu as pltpu
from jax.sharding import Mesh, PartitionSpec as P

D = 1024
K = 64
EPS = 1e-06
NY, NZ, NC, NX = 4, 8, 2, 4
PARENTS = NY * NZ * NC
ROWS = 2048
WIDTH = 256
PIECE = NZ * K
BLOCK = 512
VMEM = 40 * 1024 * 1024

F32 = jnp.float32
BF16 = jnp.bfloat16


def call(kernel, out_shape, flops, n_bytes, n_smem, n_vmem):
    smem = pl.BlockSpec(memory_space=pltpu.SMEM)
    vmem = pl.BlockSpec(memory_space=pltpu.VMEM)
    return pl.pallas_call(
        kernel,
        out_shape=out_shape,
        in_specs=[smem] * n_smem + [vmem] * n_vmem,
        out_specs=jax.tree.map(lambda _: vmem, out_shape),
        compiler_params=pltpu.CompilerParams(vmem_limit_bytes=VMEM),
        cost_estimate=pl.CostEstimate(flops=flops, bytes_accessed=n_bytes, transcendentals=0),
    )


def sums_kernel(where_ref, code_ref, other_code_ref, rows_ref, other_rows_ref, out_ref):
    y, core = where_ref[0], where_ref[1]
    total = jnp.zeros((PIECE, WIDTH), F32)
    for codes, rows in ((code_ref, rows_ref), (other_code_ref, other_rows_ref)):
        for start in range(0, ROWS, BLOCK):
            code = codes[:, start : start + BLOCK]
            parent = code >> 6
            inside = ((parent >> 4) == y) & ((parent & 1) == core)
            local = jnp.where(inside, ((parent >> 1) & 7) * K + (code & 63), -1)
            child = lax.broadcasted_iota(jnp.int32, (PIECE, BLOCK), 0)
            member = (child == local).astype(F32).astype(BF16)
            total += jnp.dot(member, rows[start : start + BLOCK, :], preferred_element_type=F32)
    out_ref[...] = total.astype(out_ref.dtype)


def merge_kernel(own_ref, a_ref, b_ref, c_ref, out_ref):
    total = own_ref[...] + a_ref[...].astype(F32) + b_ref[...].astype(F32) + c_ref[...].astype(F32)
    out_ref[...] = total.astype(BF16)


def totals_kernel(parts_ref, totals_ref, copies_ref):
    total = parts_ref[0:K, :].astype(F32)
    for z in range(1, NZ):
        total += parts_ref[z * K : (z + 1) * K, :].astype(F32)
    totals_ref[...] = total
    rounded = total.astype(BF16)
    for z in range(NZ):
        copies_ref[z * K : (z + 1) * K, :] = rounded


def scores_kernel(where_ref, parent_ref, rows_ref, *refs):
    own_refs, other_refs, out_ref = refs[:NY], refs[NY : 2 * NY], refs[2 * NY]
    y, core = where_ref[0], where_ref[1]
    lane = lax.broadcasted_iota(jnp.int32, (K, PARENTS), 1)
    squares = jnp.zeros((K, PARENTS), F32)
    for step in range(NY):
        source = (y + NY - step) & (NY - 1)
        for side, refs_of_side in ((core, own_refs), (1 - core, other_refs)):
            for z in range(NZ):
                number = source * 16 + z * 2 + side
                block = refs_of_side[step][z * K : (z + 1) * K, :].astype(F32)
                square = jnp.sum(block * block, axis=1, keepdims=True)
                squares = jnp.where(lane == number, square, squares)
    high = squares.astype(BF16)
    low = (squares - high.astype(F32)).astype(BF16)
    out_ref[:, ROWS : ROWS + PARENTS] = high
    out_ref[:, ROWS + PARENTS : ROWS + 2 * PARENTS] = low
    for start in range(0, ROWS, BLOCK):
        rows = rows_ref[start : start + BLOCK, :]
        parent = parent_ref[:, start : start + BLOCK]
        best = jnp.zeros((K, BLOCK), F32)
        for step in range(NY):
            source = (y + NY - step) & (NY - 1)
            for side, refs_of_side in ((core, own_refs), (1 - core, other_refs)):
                product = lax.dot_general(
                    refs_of_side[step][...], rows, (((1,), (1,)), ((), ())), preferred_element_type=F32
                )
                for z in range(NZ):
                    number = source * 16 + z * 2 + side
                    best = jnp.where(parent == number, product[z * K : (z + 1) * K, :], best)
        out_ref[:, start : start + BLOCK] = best.astype(BF16)


def finish_kernel(where_ref, parent_ref, a_ref, b_ref, c_ref, d_ref, totals_ref, centroids_ref, fit_ref):
    y, core, z = where_ref[0], where_ref[1], where_ref[2]
    refs = (a_ref, b_ref, c_ref, d_ref)

    def added(start, size):
        parts = [ref[:, start : start + size].astype(F32) for ref in refs]
        return (parts[0] + parts[1]) + (parts[2] + parts[3])

    squares = added(ROWS, 2 * PARENTS)
    squares = squares[:, :PARENTS] + squares[:, PARENTS:]
    scale = lax.rsqrt(squares / D + EPS)
    lane = lax.broadcasted_iota(jnp.int32, (K, PARENTS), 1)
    own = jnp.sum(jnp.where(lane == y * 16 + z * 2 + core, scale, 0.0), axis=1, keepdims=True)
    centroids_ref[...] = (totals_ref[...] * own).astype(BF16)
    high = scale.astype(BF16)
    low = (scale - high.astype(F32)).astype(BF16)
    for start in range(0, ROWS, BLOCK):
        parent = parent_ref[:, start : start + BLOCK]
        number = lax.broadcasted_iota(jnp.int32, (PARENTS, BLOCK), 0)
        chosen = (number == parent).astype(F32).astype(BF16)
        factor = jnp.dot(high, chosen, preferred_element_type=F32) + jnp.dot(
            low, chosen, preferred_element_type=F32
        )
        scores = added(start, BLOCK) * factor
        fit_ref[:, start : start + BLOCK] = jnp.max(scores, axis=0, keepdims=True) / (0.25 * D)


def shift(x, axis, size, by):
    return lax.ppermute(x, axis, [(i, (i + by) % size) for i in range(size)])


def body(embeddings, parent_ids, child_assignment):
    y, z, core = lax.axis_index("y"), lax.axis_index("z"), lax.axis_index("core")
    parent = parent_ids.reshape(1, ROWS)
    code = parent * K + child_assignment.reshape(1, ROWS)
    other_rows = shift(embeddings, "core", NC, 1)
    other_code = shift(code, "core", NC, 1)

    def sums(by, dtype):
        where = jnp.stack([(y + by) % NY, core])
        return call(
            sums_kernel, jax.ShapeDtypeStruct((PIECE, WIDTH), dtype), 2 * PIECE * WIDTH * 2 * ROWS, 3 << 20, 1, 4
        )(where, code, other_code, embeddings, other_rows)

    arrived = [shift(sums(by, BF16), "y", NY, by) for by in (2, 1, 3)]
    merged = call(merge_kernel, jax.ShapeDtypeStruct((PIECE, WIDTH), BF16), 0, 2 << 20, 0, 4)(
        sums(0, F32), *arrived
    )
    parts = lax.all_to_all(merged, "z", 0, 0, tiled=True)
    totals, copies = call(
        totals_kernel,
        (jax.ShapeDtypeStruct((K, WIDTH), F32), jax.ShapeDtypeStruct((PIECE, WIDTH), BF16)),
        0, 1 << 20, 0, 1,
    )(parts)
    mine = lax.all_to_all(copies, "z", 0, 0, tiled=True)
    far = shift(mine, "y", NY, 2)
    own_side = [mine, shift(mine, "y", NY, 1), far, shift(mine, "y", NY, 3)]
    other_side = [shift(piece, "core", NC, 1) for piece in own_side]
    where = jnp.stack([y, core, z])
    partial = call(
        scores_kernel, jax.ShapeDtypeStruct((K, ROWS + 2 * PARENTS), BF16), 2 * ROWS * 4096 * WIDTH, 4 << 20, 1, 10
    )(where, parent, embeddings, *own_side, *other_side)
    partials = [partial] + [shift(partial, "feat", NX, by) for by in (2, 1, 3)]
    centroids, fit = call(
        finish_kernel,
        (jax.ShapeDtypeStruct((K, WIDTH), BF16), jax.ShapeDtypeStruct((1, ROWS), F32)),
        2 * K * PARENTS * ROWS * 2, 2 << 20, 1, 6,
    )(where, parent, *partials, totals)
    return centroids, fit.reshape(ROWS)


def solution(mesh):
    split = Mesh(mesh.devices.reshape(NY, NZ, NC, NX), ("y", "z", "core", "feat"))
    rows = ("y", "z", "core")
    in_specs = (P(rows, "feat"), P(rows, None), P(rows))
    out_specs = (P(rows, "feat"), P(rows))
    return jax.shard_map(body, mesh=split, in_specs=in_specs, out_specs=out_specs, check_vma=False)
```

```python
import functools

import jax
import jax.numpy as jnp
from jax import lax
from jax.experimental import pallas as pl
from jax.experimental.pallas import tpu as pltpu
from jax.sharding import Mesh, PartitionSpec as P

D = 1024
K = 64
EPS = 1e-06
NY, NZ, NC, NX = 4, 8, 2, 4
PARENTS = NY * NZ * NC
ROWS = 2048
WIDTH = 256
PIECE = NZ * K
HALF = PIECE // 2
SPLIT = ROWS // 2
BLOCK = 512
VMEM = 24 * 1024 * 1024
LONG = 1 << 32

F32 = jnp.float32
BF16 = jnp.bfloat16


def call(kernel, out_shape, operands, behind=(), flops=1000, far=0, scratch=()):
    vmem = pl.BlockSpec(memory_space=pltpu.VMEM)
    hbm = pl.BlockSpec(memory_space=pltpu.HBM)
    count = len(operands)

    def skipping(*refs):
        kernel(*refs[:count], *refs[count + len(behind) :])

    return pl.pallas_call(
        skipping,
        out_shape=out_shape,
        in_specs=[hbm] * far + [vmem] * (count - far + len(behind)),
        out_specs=jax.tree.map(lambda _: vmem, out_shape),
        scratch_shapes=list(scratch),
        compiler_params=pltpu.CompilerParams(vmem_limit_bytes=VMEM),
        cost_estimate=pl.CostEstimate(flops=flops, bytes_accessed=1000, transcendentals=0),
    )(*operands, *behind)


def add_members(totals, halves, parents, children, rows, start):
    y, core = lax.axis_index("y"), lax.axis_index("core")
    span = slice(start, start + BLOCK)
    parent = parents[:, span]
    block = rows[span, :]
    child = lax.broadcasted_iota(jnp.int32, (HALF, BLOCK), 0)
    for number, (k, upper) in enumerate(halves):
        inside = ((parent >> 4) == (y ^ k)) & ((parent & 1) == core)
        local = jnp.where(inside, ((parent >> 1) & 7) * K + children[:, span] - upper * HALF, -1)
        member = (child == local).astype(F32).astype(BF16)
        totals[number] += jnp.dot(member, block, preferred_element_type=F32)


def sums_kernel(halves, groups, *refs):
    outs, so_far = refs[-len(halves) :], refs[3 * groups : -len(halves)]
    totals = [x[...].astype(F32) for x in so_far] or [jnp.zeros((HALF, WIDTH), F32) for _ in halves]
    for group in range(groups):
        for start in range(0, ROWS, BLOCK):
            add_members(totals, halves, *refs[3 * group : 3 * group + 3], start)
    for out, total in zip(outs, totals):
        out[...] = total.astype(out.dtype)


def first_sums_kernel(halves, parents_ref, children_ref, rows_ref, *refs):
    outs = refs[: len(halves)]
    parents, children, rows, sems = refs[len(halves) :]
    copies = [
        pltpu.make_async_copy(parents_ref, parents, sems.at[0]),
        pltpu.make_async_copy(children_ref, children, sems.at[1]),
    ]
    for number, start in enumerate(range(0, ROWS, BLOCK)):
        span = pl.ds(start, BLOCK)
        copies.append(pltpu.make_async_copy(rows_ref.at[span], rows.at[span], sems.at[2 + number]))
    for copy in copies:
        copy.start()
    copies[0].wait()
    copies[1].wait()
    totals = [jnp.zeros((HALF, WIDTH), F32) for _ in halves]
    for number, start in enumerate(range(0, ROWS, BLOCK)):
        copies[2 + number].wait()
        add_members(totals, halves, parents, children, rows, start)
    for out, total in zip(outs, totals):
        out[...] = total


def merge_kernel(low_ref, high_ref, low_a, low_b, high_a, high_b, out_ref):
    out_ref[:HALF, :] = (low_ref[...] + low_a[...].astype(F32) + low_b[...].astype(F32)).astype(BF16)
    out_ref[HALF:, :] = (high_ref[...] + high_a[...].astype(F32) + high_b[...].astype(F32)).astype(BF16)


def totals_kernel(parts_ref, totals_ref, copies_ref):
    total = parts_ref[0:K, :].astype(F32)
    for z in range(1, NZ):
        total += parts_ref[z * K : (z + 1) * K, :].astype(F32)
    totals_ref[...] = total
    rounded = total.astype(BF16)
    for z in range(NZ):
        copies_ref[z * K : (z + 1) * K, :] = rounded


def scores_kernel(groups, blocks, first, with_squares, *refs):
    y, core = lax.axis_index("y"), lax.axis_index("core")
    group_refs, refs = refs[: 2 * groups], refs[2 * groups :]
    block_refs, refs = refs[: len(blocks)], refs[len(blocks) :]
    numbers = [(y ^ k) * 16 + 2 * z + core for k, z, _ in blocks]
    scores_in = squares_in = None
    if not first:
        scores_in, refs = refs[:groups], refs[groups:]
        if with_squares:
            squares_in, refs = refs[0], refs[1:]
    if with_squares:
        lane = lax.broadcasted_iota(jnp.int32, (K, PARENTS), 1)
        squares = jnp.zeros((K, PARENTS), F32) if first else squares_in[...]
        for number, block_ref, (_, _, count) in zip(numbers, block_refs, blocks):
            for z in range(count):
                block = block_ref[z * K : (z + 1) * K, :].astype(F32)
                square = jnp.sum(block * block, axis=1, keepdims=True)
                squares = jnp.where(lane == number + 2 * z, square, squares)
        refs[groups][...] = squares
    for group in range(groups):
        parents, rows_ref = group_refs[2 * group : 2 * group + 2]
        for start in range(0, ROWS, BLOCK):
            span = slice(start, start + BLOCK)
            rows, parent = rows_ref[span, :], parents[:, span]
            chosen = jnp.zeros((K, BLOCK), F32) if first else scores_in[group][:, span].astype(F32)
            for number, block_ref, (_, _, count) in zip(numbers, block_refs, blocks):
                product = lax.dot_general(
                    block_ref[...], rows, (((1,), (1,)), ((), ())), preferred_element_type=F32
                )
                for z in range(count):
                    chosen = jnp.where(parent == number + 2 * z, product[z * K : (z + 1) * K, :], chosen)
            refs[group][:, span] = chosen.astype(BF16)


def put_squares(out_ref, squares):
    high = squares.astype(BF16)
    out_ref[:, SPLIT : SPLIT + PARENTS] = high
    out_ref[:, SPLIT + PARENTS :] = (squares - high.astype(F32)).astype(BF16)


def get_squares(ref):
    return ref[:, SPLIT : SPLIT + PARENTS].astype(F32) + ref[:, SPLIT + PARENTS :].astype(F32)


def join_kernel(own_ref, arrived_ref, squares_ref, other_squares_ref, a_ref, b_ref):
    a_ref[...] = own_ref[:, :SPLIT] + arrived_ref[:, :SPLIT]
    b_ref[:, :SPLIT] = own_ref[:, SPLIT:] + arrived_ref[:, SPLIT:]
    put_squares(b_ref, squares_ref[...] + other_squares_ref[...])


def add_kernel(x_ref, y_ref, out_ref):
    scores = x_ref[:, :SPLIT].astype(F32) + y_ref[:, :SPLIT].astype(F32)
    out_ref[:, :SPLIT] = scores.astype(BF16)
    if out_ref.shape[1] > SPLIT:
        put_squares(out_ref, get_squares(x_ref) + get_squares(y_ref))


def finish_kernel(parent_ref, a_ref, other_a_ref, b_ref, other_b_ref, totals_ref, centroids_ref, fit_ref):
    y, z, core = lax.axis_index("y"), lax.axis_index("z"), lax.axis_index("core")
    scale = lax.rsqrt((get_squares(b_ref) + get_squares(other_b_ref)) / D + EPS)
    lane = lax.broadcasted_iota(jnp.int32, (K, PARENTS), 1)
    own = jnp.sum(jnp.where(lane == y * 16 + z * 2 + core, scale, 0.0), axis=1, keepdims=True)
    centroids_ref[...] = (totals_ref[...] * own).astype(BF16)
    high = scale.astype(BF16)
    low = (scale - high.astype(F32)).astype(BF16)
    for start in range(0, ROWS, BLOCK):
        parent = parent_ref[:, start : start + BLOCK]
        number = lax.broadcasted_iota(jnp.int32, (PARENTS, BLOCK), 0)
        chosen = (number == parent).astype(F32).astype(BF16)
        factor = jnp.dot(high, chosen, preferred_element_type=F32) + jnp.dot(
            low, chosen, preferred_element_type=F32
        )
        x_ref, y_ref = (a_ref, other_a_ref) if start < SPLIT else (b_ref, other_b_ref)
        at = start % SPLIT
        scores = x_ref[:, at : at + BLOCK].astype(F32) + y_ref[:, at : at + BLOCK].astype(F32)
        fit_ref[:, start : start + BLOCK] = jnp.max(scores * factor, axis=0, keepdims=True) / (0.25 * D)


def swap(x):
    return lax.ppermute(x, "core", [(0, 1), (1, 0)])


def left(x, axis):
    return lax.ppermute(x, axis, [(0, 1), (1, 0), (2, 3), (3, 2)])


def right(x, axis):
    return lax.ppermute(x, axis, [(0, 3), (3, 0), (1, 2), (2, 1)])


def body(embeddings, parent_ids, child_assignment):
    own = (parent_ids.reshape(1, ROWS), child_assignment.reshape(1, ROWS), embeddings)
    other = tuple(swap(x) for x in own)

    def halves_of(dtype):
        return (jax.ShapeDtypeStruct((HALF, WIDTH), dtype),) * 2

    def sums(halves, dtype, groups, so_far=(), behind=(), flops=1000):
        return call(
            functools.partial(sums_kernel, halves, len(groups)),
            halves_of(dtype),
            [x for group in groups for x in group] + list(so_far),
            behind=behind,
            flops=flops,
        )

    halves = ((2, 0), (2, 1))
    started = call(
        functools.partial(first_sums_kernel, halves),
        halves_of(F32),
        list(own),
        far=3,
        scratch=[
            pltpu.VMEM((1, ROWS), jnp.int32),
            pltpu.VMEM((1, ROWS), jnp.int32),
            pltpu.VMEM((ROWS, WIDTH), BF16),
            pltpu.SemaphoreType.DMA((2 + ROWS // BLOCK,)),
        ],
    )
    far_low, far_high = sums(halves, BF16, [other], started)
    got_low, got_high = left(far_low, "y"), right(far_high, "y")
    left_low, right_high = sums(((1, 0), (3, 1)), BF16, [own, other], behind=[far_low, far_high], flops=LONG)
    left_high, right_low = sums(
        ((1, 1), (3, 0)), BF16, [own, other], [got_high, got_low], behind=[left_low, right_high]
    )
    kept = sums(((0, 0), (0, 1)), F32, [own, other], behind=[left_high, right_low])
    merged = call(
        merge_kernel,
        jax.ShapeDtypeStruct((PIECE, WIDTH), BF16),
        [*kept, left(left_low, "y"), right(right_low, "y"), left(left_high, "y"), right(right_high, "y")],
    )
    parts = lax.all_to_all(merged, "z", 0, 0, tiled=True)
    totals, copies = call(
        totals_kernel,
        (jax.ShapeDtypeStruct((K, WIDTH), F32), jax.ShapeDtypeStruct((PIECE, WIDTH), BF16)),
        [parts],
    )
    mine = lax.all_to_all(copies, "z", 0, 0, tiled=True)

    low, high = mine[:HALF], mine[HALF:]
    left_low, right_high = left(low, "y"), right(high, "y")
    left_high, right_low = left(high, "y"), right(low, "y")
    far_low, far_high = right(left_low, "y"), left(right_high, "y")

    own_rows, other_rows = [own[0], own[2]], [other[0], other[2]]
    plain = jax.ShapeDtypeStruct((K, ROWS), BF16)
    squared = jax.ShapeDtypeStruct((K, PARENTS), F32)
    state = call(
        functools.partial(scores_kernel, 2, ((0, 0, NZ),), True, True),
        (plain, plain, squared),
        [*own_rows, *other_rows, mine],
    )
    blocks = ((1, 0, 4), (1, 4, 4), (3, 0, 4), (3, 4, 4))
    state = call(
        functools.partial(scores_kernel, 2, blocks, False, True),
        (plain, plain, squared),
        [*own_rows, *other_rows, left_low, left_high, right_low, right_high, *state],
        flops=LONG,
    )
    blocks = ((2, 0, 4), (2, 4, 4))
    sent, squares = call(
        functools.partial(scores_kernel, 1, blocks, False, True),
        (plain, squared),
        [*other_rows, far_low, far_high, *state[1:]],
    )
    (kept,) = call(
        functools.partial(scores_kernel, 1, blocks, False, False),
        (plain,),
        [*own_rows, far_low, far_high, state[0]],
        behind=[sent],
    )
    message = jax.ShapeDtypeStruct((K, SPLIT), BF16)
    long_message = jax.ShapeDtypeStruct((K, SPLIT + 2 * PARENTS), BF16)
    a, b = call(join_kernel, (message, long_message), [kept, swap(sent), squares, swap(squares)])

    a = call(add_kernel, message, [a, left(a, "feat")])
    b = call(add_kernel, long_message, [b, right(b, "feat")])
    centroids, fit = call(
        finish_kernel,
        (jax.ShapeDtypeStruct((K, WIDTH), BF16), jax.ShapeDtypeStruct((1, ROWS), F32)),
        [own[0], a, right(a, "feat"), b, left(b, "feat"), totals],
    )
    return centroids, fit.reshape(ROWS)


def solution(mesh):
    split = Mesh(mesh.devices.reshape(NY, NZ, NC, NX), ("y", "z", "core", "feat"))
    rows = ("y", "z", "core")
    in_specs = (P(rows, "feat"), P(rows, None), P(rows))
    out_specs = (P(rows, "feat"), P(rows))
    return jax.shard_map(body, mesh=split, in_specs=in_specs, out_specs=out_specs, check_vma=False)
```

```python
import functools

import jax
import jax.numpy as jnp
from jax import lax
from jax.experimental import pallas as pl
from jax.experimental.pallas import tpu as pltpu
from jax.sharding import Mesh, PartitionSpec as P

D = 1024
K = 64
EPS = 1e-06
NY, NZ, NC, NX = 4, 8, 2, 4
PARENTS = NY * NZ * NC
ROWS = 2048
WIDTH = 256
PIECE = NZ * K
HALF = PIECE // 2
SPLIT = ROWS // 2
BLOCK = 512
VMEM = 24 * 1024 * 1024
LONG = 1 << 32

F32 = jnp.float32
BF16 = jnp.bfloat16


def call(kernel, out_shape, operands, behind=(), flops=1000):
    vmem = pl.BlockSpec(memory_space=pltpu.VMEM)
    count = len(operands)

    def skipping(*refs):
        kernel(*refs[:count], *refs[count + len(behind) :])

    return pl.pallas_call(
        skipping,
        out_shape=out_shape,
        in_specs=[vmem] * (count + len(behind)),
        out_specs=jax.tree.map(lambda _: vmem, out_shape),
        compiler_params=pltpu.CompilerParams(vmem_limit_bytes=VMEM),
        cost_estimate=pl.CostEstimate(flops=flops, bytes_accessed=1000, transcendentals=0),
    )(*operands, *behind)


def add_members(totals, halves, codes, rows, start):
    y, core = lax.axis_index("y"), lax.axis_index("core")
    span = slice(start, start + BLOCK)
    code = codes[:, span]
    parent = code >> 6
    block = rows[span, :]
    child = lax.broadcasted_iota(jnp.int32, (HALF, BLOCK), 0)
    for number, (k, upper) in enumerate(halves):
        inside = ((parent >> 4) == (y ^ k)) & ((parent & 1) == core)
        local = jnp.where(inside, ((parent >> 1) & 7) * K + (code & (K - 1)) - upper * HALF, -1)
        member = (child == local).astype(F32).astype(BF16)
        totals[number] += jnp.dot(member, block, preferred_element_type=F32)


def sums_kernel(halves, groups, *refs):
    outs, so_far = refs[-len(halves) :], refs[2 * groups : -len(halves)]
    totals = [x[...].astype(F32) for x in so_far] or [jnp.zeros((HALF, WIDTH), F32) for _ in halves]
    for group in range(groups):
        for start in range(0, ROWS, BLOCK):
            add_members(totals, halves, *refs[2 * group : 2 * group + 2], start)
    for out, total in zip(outs, totals):
        out[...] = total.astype(out.dtype)


def hand_on_kernel(own_ref, got_ref, out_ref):
    out_ref[...] = (own_ref[...] + got_ref[...].astype(F32)).astype(BF16)


def merge_kernel(low_ref, high_ref, low_a, low_b, high_a, high_b, out_ref):
    out_ref[:HALF, :] = (low_ref[...] + low_a[...].astype(F32) + low_b[...].astype(F32)).astype(BF16)
    out_ref[HALF:, :] = (high_ref[...] + high_a[...].astype(F32) + high_b[...].astype(F32)).astype(BF16)


def totals_kernel(parts_ref, totals_ref, copies_ref):
    total = parts_ref[0:K, :].astype(F32)
    for z in range(1, NZ):
        total += parts_ref[z * K : (z + 1) * K, :].astype(F32)
    totals_ref[...] = total
    rounded = total.astype(BF16)
    for z in range(NZ):
        copies_ref[z * K : (z + 1) * K, :] = rounded


def scores_kernel(groups, blocks, first, with_squares, packed, span, *refs):
    y, core = lax.axis_index("y"), lax.axis_index("core")
    group_refs, refs = refs[: 2 * groups], refs[2 * groups :]
    block_refs, refs = refs[: len(blocks)], refs[len(blocks) :]
    numbers = [(y ^ k) * 16 + 2 * z + core for k, z, _ in blocks]
    scores_in = squares_in = None
    if not first:
        scores_in, refs = refs[:groups], refs[groups:]
        if with_squares:
            squares_in, refs = refs[0], refs[1:]
    if with_squares:
        lane = lax.broadcasted_iota(jnp.int32, (K, PARENTS), 1)
        squares = jnp.zeros((K, PARENTS), F32) if first else squares_in[...]
        for number, block_ref, (_, _, count) in zip(numbers, block_refs, blocks):
            for z in range(count):
                block = block_ref[z * K : (z + 1) * K, :].astype(F32)
                square = jnp.sum(block * block, axis=1, keepdims=True)
                squares = jnp.where(lane == number + 2 * z, square, squares)
        if packed:
            put_squares(refs[0], squares, SPLIT)
        else:
            refs[groups][...] = squares
    for group in range(groups):
        codes, rows_ref = group_refs[2 * group : 2 * group + 2]
        for start in range(*span, BLOCK):
            part = slice(start, start + BLOCK)
            rows, parent = rows_ref[part, :], codes[:, part] >> 6
            chosen = jnp.zeros((K, BLOCK), F32) if first else scores_in[group][:, part].astype(F32)
            for number, block_ref, (_, _, count) in zip(numbers, block_refs, blocks):
                product = lax.dot_general(
                    block_ref[...], rows, (((1,), (1,)), ((), ())), preferred_element_type=F32
                )
                for z in range(count):
                    chosen = jnp.where(parent == number + 2 * z, product[z * K : (z + 1) * K, :], chosen)
            refs[group][:, start - span[0] : start - span[0] + BLOCK] = chosen.astype(BF16)


def put_squares(out_ref, squares, at):
    high = squares.astype(BF16)
    out_ref[:, at : at + PARENTS] = high
    out_ref[:, at + PARENTS : at + 2 * PARENTS] = (squares - high.astype(F32)).astype(BF16)


def get_squares(ref, at):
    return ref[:, at : at + PARENTS].astype(F32) + ref[:, at + PARENTS : at + 2 * PARENTS].astype(F32)


def join_kernel(own_ref, sent_ref, arrived_ref, out_ref):
    out_ref[:, :SPLIT] = own_ref[...] + arrived_ref[:, :SPLIT]
    if out_ref.shape[1] > SPLIT:
        out_ref[:, SPLIT:] = sent_ref[:, SPLIT:] + arrived_ref[:, SPLIT:]


def add_kernel(x_ref, y_ref, out_ref):
    scores = x_ref[:, :SPLIT].astype(F32) + y_ref[:, :SPLIT].astype(F32)
    out_ref[:, :SPLIT] = scores.astype(BF16)
    if out_ref.shape[1] > SPLIT:
        put_squares(out_ref, get_squares(x_ref, SPLIT) + get_squares(y_ref, SPLIT), SPLIT)


def best_rows(code_ref, at, x_ref, y_ref, scale, fit_ref):
    high = scale.astype(BF16)
    low = (scale - high.astype(F32)).astype(BF16)
    for start in range(0, SPLIT, BLOCK):
        part = slice(start, start + BLOCK)
        parent = code_ref[:, at + start : at + start + BLOCK] >> 6
        number = lax.broadcasted_iota(jnp.int32, (PARENTS, BLOCK), 0)
        chosen = (number == parent).astype(F32).astype(BF16)
        factor = jnp.dot(high, chosen, preferred_element_type=F32) + jnp.dot(
            low, chosen, preferred_element_type=F32
        )
        scores = x_ref[:, part].astype(F32) + y_ref[:, part].astype(F32)
        fit_ref[:, at + start : at + start + BLOCK] = jnp.max(scores * factor, axis=0, keepdims=True) / (
            0.25 * D
        )


def finish_first_kernel(code_ref, x_ref, y_ref, totals_ref, scale_ref, centroids_ref, fit_ref):
    y, z, core = lax.axis_index("y"), lax.axis_index("z"), lax.axis_index("core")
    scale = lax.rsqrt((get_squares(x_ref, SPLIT) + get_squares(y_ref, SPLIT)) / D + EPS)
    scale_ref[...] = scale
    lane = lax.broadcasted_iota(jnp.int32, (K, PARENTS), 1)
    own = jnp.sum(jnp.where(lane == y * 16 + z * 2 + core, scale, 0.0), axis=1, keepdims=True)
    centroids_ref[...] = (totals_ref[...] * own).astype(BF16)
    best_rows(code_ref, 0, x_ref, y_ref, scale, fit_ref)


def finish_kernel(code_ref, x_ref, y_ref, scale_ref, first_ref, fit_ref):
    fit_ref[:, :SPLIT] = first_ref[...]
    best_rows(code_ref, SPLIT, x_ref, y_ref, scale_ref[...], fit_ref)


def swap(x):
    return lax.ppermute(x, "core", [(0, 1), (1, 0)])


def left(x, axis):
    return lax.ppermute(x, axis, [(0, 1), (1, 0), (2, 3), (3, 2)])


def right(x, axis):
    return lax.ppermute(x, axis, [(0, 3), (3, 0), (1, 2), (2, 1)])


def body(embeddings, parent_ids, child_assignment):
    code = parent_ids.reshape(1, ROWS) * K + child_assignment.reshape(1, ROWS)
    own = (code, embeddings)
    other = tuple(swap(x) for x in own)

    def halves_of(dtype):
        return (jax.ShapeDtypeStruct((HALF, WIDTH), dtype),) * 2

    def sums(halves, dtype, groups, so_far=(), behind=(), flops=1000):
        return call(
            functools.partial(sums_kernel, halves, len(groups)),
            halves_of(dtype),
            [x for group in groups for x in group] + list(so_far),
            behind=behind,
            flops=flops,
        )

    halves = ((2, 0), (2, 1))
    far_low, far_high = sums(halves, BF16, [other], sums(halves, F32, [own]))
    got_low, got_high = left(far_low, "y"), right(far_high, "y")
    left_low, right_high = sums(((1, 0), (3, 1)), BF16, [own, other], behind=[far_low, far_high], flops=LONG)
    own_high, own_low = sums(((1, 1), (3, 0)), F32, [own, other], behind=[left_low, right_high])
    half = jax.ShapeDtypeStruct((HALF, WIDTH), BF16)
    right_low = call(hand_on_kernel, half, [own_low, got_low])
    left_high = call(hand_on_kernel, half, [own_high, got_high])
    kept = sums(((0, 0), (0, 1)), F32, [own, other], behind=[left_high, right_low])
    merged = call(
        merge_kernel,
        jax.ShapeDtypeStruct((PIECE, WIDTH), BF16),
        [*kept, left(left_low, "y"), right(right_low, "y"), left(left_high, "y"), right(right_high, "y")],
    )
    parts = lax.all_to_all(merged, "z", 0, 0, tiled=True)
    totals, copies = call(
        totals_kernel,
        (jax.ShapeDtypeStruct((K, WIDTH), F32), jax.ShapeDtypeStruct((PIECE, WIDTH), BF16)),
        [parts],
    )
    mine = lax.all_to_all(copies, "z", 0, 0, tiled=True)

    low, high = mine[:HALF], mine[HALF:]
    left_low, right_high = left(low, "y"), right(high, "y")
    left_high, right_low = left(high, "y"), right(low, "y")
    far_low, far_high = right(left_low, "y"), left(right_high, "y")

    plain = jax.ShapeDtypeStruct((K, ROWS), BF16)
    squared = jax.ShapeDtypeStruct((K, PARENTS), F32)
    blocks = ((0, 0, NZ), (1, 0, 4), (1, 4, 4), (3, 0, 4), (3, 4, 4))
    state = call(
        functools.partial(scores_kernel, 2, blocks, True, True, False, (0, ROWS)),
        (plain, plain, squared),
        [*own, *other, mine, left_low, left_high, right_low, right_high],
        flops=LONG,
    )
    blocks = ((2, 0, 4), (2, 4, 4))
    message = jax.ShapeDtypeStruct((K, SPLIT), BF16)
    long_message = jax.ShapeDtypeStruct((K, SPLIT + 2 * PARENTS), BF16)
    spans = ((0, SPLIT), (SPLIT, ROWS))
    (sent_a,) = call(
        functools.partial(scores_kernel, 1, blocks, False, True, True, spans[0]),
        (long_message,),
        [*other, far_low, far_high, *state[1:]],
    )
    (sent_b,) = call(
        functools.partial(scores_kernel, 1, blocks, False, False, False, spans[1]),
        (message,),
        [*other, far_low, far_high, state[1]],
        behind=[sent_a],
    )
    got_a, got_b = swap(sent_a), swap(sent_b)
    (kept_a,) = call(
        functools.partial(scores_kernel, 1, blocks, False, False, False, spans[0]),
        (message,),
        [*own, far_low, far_high, state[0]],
        behind=[sent_b],
    )
    a = call(join_kernel, long_message, [kept_a, sent_a, got_a])
    (kept_b,) = call(
        functools.partial(scores_kernel, 1, blocks, False, False, False, spans[1]),
        (message,),
        [*own, far_low, far_high, state[0]],
        behind=[a],
    )
    b = call(join_kernel, message, [kept_b, sent_b, got_b])

    a = call(add_kernel, long_message, [a, left(a, "feat")])
    b = call(add_kernel, message, [b, right(b, "feat")])
    scale, centroids, first = call(
        finish_first_kernel,
        (
            jax.ShapeDtypeStruct((K, PARENTS), F32),
            jax.ShapeDtypeStruct((K, WIDTH), BF16),
            jax.ShapeDtypeStruct((1, SPLIT), F32),
        ),
        [code, a, right(a, "feat"), totals],
    )
    fit = call(
        finish_kernel, jax.ShapeDtypeStruct((1, ROWS), F32), [code, b, left(b, "feat"), scale, first]
    )
    return centroids, fit.reshape(ROWS)


def solution(mesh):
    split = Mesh(mesh.devices.reshape(NY, NZ, NC, NX), ("y", "z", "core", "feat"))
    rows = ("y", "z", "core")
    in_specs = (P(rows, "feat"), P(rows, None), P(rows))
    out_specs = (P(rows, "feat"), P(rows))
    return jax.shard_map(body, mesh=split, in_specs=in_specs, out_specs=out_specs, check_vma=False)
```

```python
import functools

import jax
import jax.numpy as jnp
from jax import lax
from jax.experimental import pallas as pl
from jax.experimental.pallas import tpu as pltpu
from jax.sharding import Mesh, PartitionSpec as P

D = 1024
K = 64
EPS = 1e-06
NY, NZ, NC, NX = 4, 8, 2, 4
PARENTS = NY * NZ * NC
ROWS = 2048
WIDTH = 256
PIECE = NZ * K
HALF = PIECE // 2
SPLIT = ROWS // 2
BLOCK = 512
VMEM = 24 * 1024 * 1024
LONG = 1 << 32

F32 = jnp.float32
BF16 = jnp.bfloat16


def call(kernel, out_shape, operands, behind=(), flops=1000):
    vmem = pl.BlockSpec(memory_space=pltpu.VMEM)
    count = len(operands)

    def skipping(*refs):
        kernel(*refs[:count], *refs[count + len(behind) :])

    return pl.pallas_call(
        skipping,
        out_shape=out_shape,
        in_specs=[vmem] * (count + len(behind)),
        out_specs=jax.tree.map(lambda _: vmem, out_shape),
        compiler_params=pltpu.CompilerParams(vmem_limit_bytes=VMEM),
        cost_estimate=pl.CostEstimate(flops=flops, bytes_accessed=1000, transcendentals=0),
    )(*operands, *behind)


def add_members(totals, halves, codes, rows, start):
    y, core = lax.axis_index("y"), lax.axis_index("core")
    span = slice(start, start + BLOCK)
    code = codes[:, span]
    parent = code >> 6
    block = rows[span, :]
    child = lax.broadcasted_iota(jnp.int32, (HALF, BLOCK), 0)
    for number, (k, upper) in enumerate(halves):
        inside = ((parent >> 4) == (y ^ k)) & ((parent & 1) == core)
        local = jnp.where(inside, ((parent >> 1) & 7) * K + (code & (K - 1)) - upper * HALF, -1)
        member = (child == local).astype(F32).astype(BF16)
        totals[number] += jnp.dot(member, block, preferred_element_type=F32)


def sums_kernel(halves, groups, *refs):
    outs, so_far = refs[-len(halves) :], refs[2 * groups : -len(halves)]
    totals = [x[...].astype(F32) for x in so_far] or [jnp.zeros((HALF, WIDTH), F32) for _ in halves]
    for group in range(groups):
        for start in range(0, ROWS, BLOCK):
            add_members(totals, halves, *refs[2 * group : 2 * group + 2], start)
    for out, total in zip(outs, totals):
        out[...] = total.astype(out.dtype)


def hand_on_kernel(own_ref, got_ref, out_ref):
    out_ref[...] = (own_ref[...] + got_ref[...].astype(F32)).astype(BF16)


def merge_kernel(low_ref, high_ref, low_a, low_b, high_a, high_b, out_ref):
    out_ref[:HALF, :] = (low_ref[...] + low_a[...].astype(F32) + low_b[...].astype(F32)).astype(BF16)
    out_ref[HALF:, :] = (high_ref[...] + high_a[...].astype(F32) + high_b[...].astype(F32)).astype(BF16)


def totals_kernel(parts_ref, totals_ref, copies_ref):
    total = parts_ref[0:K, :].astype(F32)
    for z in range(1, NZ):
        total += parts_ref[z * K : (z + 1) * K, :].astype(F32)
    totals_ref[...] = total
    rounded = total.astype(BF16)
    for z in range(NZ):
        copies_ref[z * K : (z + 1) * K, :] = rounded


def turned(k, core):
    return k ^ (2 * core) if k & 1 else k


def scores_kernel(groups, blocks, first, with_squares, packed, span, *refs):
    y, core = lax.axis_index("y"), lax.axis_index("core")
    group_refs, refs = refs[: 2 * groups], refs[2 * groups :]
    block_refs, refs = refs[: len(blocks)], refs[len(blocks) :]
    numbers = [(y ^ turned(k, core)) * 16 + 2 * z + core for k, z, _ in blocks]
    scores_in = squares_in = None
    if not first:
        scores_in, refs = refs[:groups], refs[groups:]
        if with_squares:
            squares_in, refs = refs[0], refs[1:]
    if with_squares:
        lane = lax.broadcasted_iota(jnp.int32, (K, PARENTS), 1)
        squares = jnp.zeros((K, PARENTS), F32) if first else squares_in[...]
        for number, block_ref, (_, _, count) in zip(numbers, block_refs, blocks):
            for z in range(count):
                block = block_ref[z * K : (z + 1) * K, :].astype(F32)
                square = jnp.sum(block * block, axis=1, keepdims=True)
                squares = jnp.where(lane == number + 2 * z, square, squares)
        if packed:
            put_squares(refs[0], squares, SPLIT)
        else:
            refs[groups][...] = squares
    for group in range(groups):
        codes, rows_ref = group_refs[2 * group : 2 * group + 2]
        for start in range(*span, BLOCK):
            part = slice(start, start + BLOCK)
            rows, parent = rows_ref[part, :], codes[:, part] >> 6
            chosen = jnp.zeros((K, BLOCK), F32) if first else scores_in[group][:, part].astype(F32)
            for number, block_ref, (_, _, count) in zip(numbers, block_refs, blocks):
                product = lax.dot_general(
                    block_ref[...], rows, (((1,), (1,)), ((), ())), preferred_element_type=F32
                )
                for z in range(count):
                    chosen = jnp.where(parent == number + 2 * z, product[z * K : (z + 1) * K, :], chosen)
            refs[group][:, start - span[0] : start - span[0] + BLOCK] = chosen.astype(BF16)


def put_squares(out_ref, squares, at):
    high = squares.astype(BF16)
    out_ref[:, at : at + PARENTS] = high
    out_ref[:, at + PARENTS : at + 2 * PARENTS] = (squares - high.astype(F32)).astype(BF16)


def get_squares(ref, at):
    return ref[:, at : at + PARENTS].astype(F32) + ref[:, at + PARENTS : at + 2 * PARENTS].astype(F32)


def join_kernel(own_ref, sent_ref, arrived_ref, out_ref):
    out_ref[:, :SPLIT] = own_ref[...] + arrived_ref[:, :SPLIT]
    if out_ref.shape[1] > SPLIT:
        out_ref[:, SPLIT:] = sent_ref[:, SPLIT:] + arrived_ref[:, SPLIT:]


def add_kernel(x_ref, y_ref, out_ref):
    scores = x_ref[:, :SPLIT].astype(F32) + y_ref[:, :SPLIT].astype(F32)
    out_ref[:, :SPLIT] = scores.astype(BF16)
    if out_ref.shape[1] > SPLIT:
        put_squares(out_ref, get_squares(x_ref, SPLIT) + get_squares(y_ref, SPLIT), SPLIT)


def factors(code, scale):
    high = scale.astype(BF16)
    low = (scale - high.astype(F32)).astype(BF16)
    number = lax.broadcasted_iota(jnp.int32, (PARENTS, BLOCK), 0)
    chosen = (number == code >> 6).astype(F32).astype(BF16)
    return jnp.dot(high, chosen, preferred_element_type=F32) + jnp.dot(
        low, chosen, preferred_element_type=F32
    )


def best(x, y, factor):
    return jnp.max((x.astype(F32) + y.astype(F32)) * factor, axis=0, keepdims=True) / (0.25 * D)


def finish_first_kernel(code_ref, x_ref, y_ref, totals_ref, factor_ref, centroids_ref, fit_ref):
    y, z, core = lax.axis_index("y"), lax.axis_index("z"), lax.axis_index("core")
    scale = lax.rsqrt((get_squares(x_ref, SPLIT) + get_squares(y_ref, SPLIT)) / D + EPS)
    lane = lax.broadcasted_iota(jnp.int32, (K, PARENTS), 1)
    own = jnp.sum(jnp.where(lane == y * 16 + z * 2 + core, scale, 0.0), axis=1, keepdims=True)
    centroids_ref[...] = (totals_ref[...] * own).astype(BF16)
    for start in range(0, SPLIT, BLOCK):
        part, later = slice(start, start + BLOCK), slice(SPLIT + start, SPLIT + start + BLOCK)
        fit_ref[:, part] = best(x_ref[:, part], y_ref[:, part], factors(code_ref[:, part], scale))
        factor_ref[:, part] = factors(code_ref[:, later], scale)


def finish_kernel(x_ref, y_ref, factor_ref, first_ref, fit_ref):
    fit_ref[:, :SPLIT] = first_ref[...]
    fit_ref[:, SPLIT:] = best(x_ref[...], y_ref[...], factor_ref[...])


def copy_kernel(x_ref, out_ref):
    out_ref[...] = x_ref[...]


def swap(x):
    return lax.ppermute(x, "core", [(0, 1), (1, 0)])


def left(x, axis):
    return lax.ppermute(x, axis, [(0, 1), (1, 0), (2, 3), (3, 2)])


def right(x, axis):
    return lax.ppermute(x, axis, [(0, 3), (3, 0), (1, 2), (2, 1)])


def turn(x, k):
    pairs = [(2 * i + core, 2 * (i ^ turned(k, core)) + core) for core in range(NC) for i in range(NY)]
    return lax.ppermute(x, ("y", "core"), pairs)


def body(embeddings, parent_ids, child_assignment):
    code = parent_ids.reshape(1, ROWS) * K + child_assignment.reshape(1, ROWS)
    code = call(copy_kernel, jax.ShapeDtypeStruct((1, ROWS), jnp.int32), [code], flops=LONG)
    own = (code, embeddings)
    other = tuple(swap(x) for x in own)

    def halves_of(dtype):
        return (jax.ShapeDtypeStruct((HALF, WIDTH), dtype),) * 2

    def sums(halves, dtype, groups, so_far=(), behind=(), flops=1000):
        return call(
            functools.partial(sums_kernel, halves, len(groups)),
            halves_of(dtype),
            [x for group in groups for x in group] + list(so_far),
            behind=behind,
            flops=flops,
        )

    halves = ((2, 0), (2, 1))
    far_low, far_high = sums(halves, BF16, [other], sums(halves, F32, [own]))
    got_low, got_high = left(far_low, "y"), right(far_high, "y")
    left_low, right_high = sums(((1, 0), (3, 1)), BF16, [own, other], behind=[far_low, far_high], flops=LONG)
    own_high, own_low = sums(((1, 1), (3, 0)), F32, [own, other], behind=[left_low, right_high])
    half = jax.ShapeDtypeStruct((HALF, WIDTH), BF16)
    right_low = call(hand_on_kernel, half, [own_low, got_low])
    left_high = call(hand_on_kernel, half, [own_high, got_high])
    kept = sums(((0, 0), (0, 1)), F32, [own, other], behind=[left_high, right_low])
    merged = call(
        merge_kernel,
        jax.ShapeDtypeStruct((PIECE, WIDTH), BF16),
        [*kept, left(left_low, "y"), right(right_low, "y"), left(left_high, "y"), right(right_high, "y")],
    )
    parts = lax.all_to_all(merged, "z", 0, 0, tiled=True)
    totals, copies = call(
        totals_kernel,
        (jax.ShapeDtypeStruct((K, WIDTH), F32), jax.ShapeDtypeStruct((PIECE, WIDTH), BF16)),
        [parts],
    )
    mine = lax.all_to_all(copies, "z", 0, 0, tiled=True)

    low, high = mine[:HALF], mine[HALF:]
    left_low, right_high = turn(low, 1), turn(high, 3)
    left_high, right_low = turn(high, 1), turn(low, 3)
    far_low, far_high = turn(left_low, 3), turn(right_high, 1)

    plain = jax.ShapeDtypeStruct((K, ROWS), BF16)
    squared = jax.ShapeDtypeStruct((K, PARENTS), F32)
    blocks = ((0, 0, NZ), (1, 0, 4), (1, 4, 4), (3, 0, 4), (3, 4, 4))
    state = call(
        functools.partial(scores_kernel, 2, blocks, True, True, False, (0, ROWS)),
        (plain, plain, squared),
        [*own, *other, mine, left_low, left_high, right_low, right_high],
        flops=LONG,
    )
    blocks = ((2, 0, 4), (2, 4, 4))
    message = jax.ShapeDtypeStruct((K, SPLIT), BF16)
    long_message = jax.ShapeDtypeStruct((K, SPLIT + 2 * PARENTS), BF16)
    spans = ((0, SPLIT), (SPLIT, ROWS))
    (sent_a,) = call(
        functools.partial(scores_kernel, 1, blocks, False, True, True, spans[0]),
        (long_message,),
        [*other, far_low, far_high, *state[1:]],
    )
    (sent_b,) = call(
        functools.partial(scores_kernel, 1, blocks, False, False, False, spans[1]),
        (message,),
        [*other, far_low, far_high, state[1]],
        behind=[sent_a],
    )
    got_a, got_b = swap(sent_a), swap(sent_b)
    (kept_a,) = call(
        functools.partial(scores_kernel, 1, blocks, False, False, False, spans[0]),
        (message,),
        [*own, far_low, far_high, state[0]],
        behind=[sent_b],
    )
    a = call(join_kernel, long_message, [kept_a, sent_a, got_a])
    (kept_b,) = call(
        functools.partial(scores_kernel, 1, blocks, False, False, False, spans[1]),
        (message,),
        [*own, far_low, far_high, state[0]],
        behind=[a],
    )
    b = call(join_kernel, message, [kept_b, sent_b, got_b])

    a = call(add_kernel, long_message, [a, left(a, "feat")])
    b = call(add_kernel, message, [b, right(b, "feat")])
    factor, centroids, first = call(
        finish_first_kernel,
        (
            jax.ShapeDtypeStruct((K, SPLIT), F32),
            jax.ShapeDtypeStruct((K, WIDTH), BF16),
            jax.ShapeDtypeStruct((1, SPLIT), F32),
        ),
        [code, a, right(a, "feat"), totals],
    )
    fit = call(
        finish_kernel, jax.ShapeDtypeStruct((1, ROWS), F32), [b, left(b, "feat"), factor, first]
    )
    return centroids, fit.reshape(ROWS)


def solution(mesh):
    split = Mesh(mesh.devices.reshape(NY, NZ, NC, NX), ("y", "z", "core", "feat"))
    rows = ("y", "z", "core")
    in_specs = (P(rows, "feat"), P(rows, None), P(rows))
    out_specs = (P(rows, "feat"), P(rows))
    return jax.shard_map(body, mesh=split, in_specs=in_specs, out_specs=out_specs, check_vma=False)
```

```python
import functools

import jax
import jax.numpy as jnp
from jax import lax
from jax.experimental import pallas as pl
from jax.experimental.pallas import tpu as pltpu
from jax.sharding import Mesh, PartitionSpec as P

D = 1024
K = 64
EPS = 1e-06
NY, NZ, NC, NX = 4, 8, 2, 4
PARENTS = NY * NZ * NC
ROWS = 2048
WIDTH = 256
PIECE = NZ * K
HALF = PIECE // 2
SPLIT = ROWS // 2
BLOCK = 512
VMEM = 24 * 1024 * 1024
LONG = 1 << 32

F32 = jnp.float32
BF16 = jnp.bfloat16


def call(kernel, out_shape, operands, behind=(), flops=1000):
    vmem = pl.BlockSpec(memory_space=pltpu.VMEM)
    count = len(operands)

    def skipping(*refs):
        kernel(*refs[:count], *refs[count + len(behind) :])

    return pl.pallas_call(
        skipping,
        out_shape=out_shape,
        in_specs=[vmem] * (count + len(behind)),
        out_specs=jax.tree.map(lambda _: vmem, out_shape),
        compiler_params=pltpu.CompilerParams(vmem_limit_bytes=VMEM),
        cost_estimate=pl.CostEstimate(flops=flops, bytes_accessed=1000, transcendentals=0),
    )(*operands, *behind)


def add_members(totals, halves, codes, rows, start):
    y, core = lax.axis_index("y"), lax.axis_index("core")
    span = slice(start, start + BLOCK)
    code = codes[:, span]
    parent = code >> 6
    block = rows[span, :]
    child = lax.broadcasted_iota(jnp.int32, (HALF, BLOCK), 0)
    for number, (k, upper) in enumerate(halves):
        inside = ((parent >> 4) == (y ^ k)) & ((parent & 1) == core)
        local = jnp.where(inside, ((parent >> 1) & 7) * K + (code & (K - 1)) - upper * HALF, -1)
        member = (child == local).astype(F32).astype(BF16)
        totals[number] += jnp.dot(member, block, preferred_element_type=F32)


def sums_kernel(halves, groups, *refs):
    outs, so_far = refs[-len(halves) :], refs[2 * groups : -len(halves)]
    totals = [x[...].astype(F32) for x in so_far] or [jnp.zeros((HALF, WIDTH), F32) for _ in halves]
    for group in range(groups):
        for start in range(0, ROWS, BLOCK):
            add_members(totals, halves, *refs[2 * group : 2 * group + 2], start)
    for out, total in zip(outs, totals):
        out[...] = total.astype(out.dtype)


def hand_on_kernel(own_ref, got_ref, out_ref):
    out_ref[...] = (own_ref[...] + got_ref[...].astype(F32)).astype(BF16)


def merge_kernel(low_ref, high_ref, low_a, low_b, high_a, high_b, out_ref):
    out_ref[:HALF, :] = (low_ref[...] + low_a[...].astype(F32) + low_b[...].astype(F32)).astype(BF16)
    out_ref[HALF:, :] = (high_ref[...] + high_a[...].astype(F32) + high_b[...].astype(F32)).astype(BF16)


def totals_kernel(parts_ref, totals_ref, copies_ref):
    total = parts_ref[0:K, :].astype(F32)
    for z in range(1, NZ):
        total += parts_ref[z * K : (z + 1) * K, :].astype(F32)
    totals_ref[...] = total
    rounded = total.astype(BF16)
    for z in range(NZ):
        copies_ref[z * K : (z + 1) * K, :] = rounded


def turned(k, core):
    return k ^ (2 * core) if k & 1 else k


def scores_kernel(groups, blocks, first, with_squares, packed, span, *refs):
    y, core = lax.axis_index("y"), lax.axis_index("core")
    group_refs, refs = refs[: 2 * groups], refs[2 * groups :]
    block_refs, refs = refs[: len(blocks)], refs[len(blocks) :]
    numbers = [(y ^ turned(k, core)) * 16 + core for k in blocks]
    scores_in = squares_in = None
    if not first:
        scores_in, refs = refs[:groups], refs[groups:]
        if with_squares:
            squares_in, refs = refs[0], refs[1:]
    if with_squares:
        lane = lax.broadcasted_iota(jnp.int32, (K, PARENTS), 1)
        squares = jnp.zeros((K, PARENTS), F32) if first else squares_in[...]
        for number, block_ref in zip(numbers, block_refs):
            for z in range(NZ):
                block = block_ref[z * K : (z + 1) * K, :].astype(F32)
                square = jnp.sum(block * block, axis=1, keepdims=True)
                squares = jnp.where(lane == number + 2 * z, square, squares)
        if packed:
            put_squares(refs[0], squares, SPLIT)
        else:
            refs[groups][...] = squares
    for group in range(groups):
        codes, rows_ref = group_refs[2 * group : 2 * group + 2]
        for start in range(*span, BLOCK):
            part = slice(start, start + BLOCK)
            rows, parent = rows_ref[part, :], codes[:, part] >> 6
            chosen = jnp.zeros((K, BLOCK), F32) if first else scores_in[group][:, part].astype(F32)
            for number, block_ref in zip(numbers, block_refs):
                product = lax.dot_general(
                    block_ref[...], rows, (((1,), (1,)), ((), ())), preferred_element_type=F32
                )
                for z in range(NZ):
                    chosen = jnp.where(parent == number + 2 * z, product[z * K : (z + 1) * K, :], chosen)
            refs[group][:, start - span[0] : start - span[0] + BLOCK] = chosen.astype(BF16)


def put_squares(out_ref, squares, at):
    high = squares.astype(BF16)
    out_ref[:, at : at + PARENTS] = high
    out_ref[:, at + PARENTS : at + 2 * PARENTS] = (squares - high.astype(F32)).astype(BF16)


def get_squares(ref, at):
    return ref[:, at : at + PARENTS].astype(F32) + ref[:, at + PARENTS : at + 2 * PARENTS].astype(F32)


def join_kernel(own_ref, sent_ref, arrived_ref, out_ref):
    out_ref[:, :SPLIT] = own_ref[...] + arrived_ref[:, :SPLIT]
    if out_ref.shape[1] > SPLIT:
        out_ref[:, SPLIT:] = sent_ref[:, SPLIT:] + arrived_ref[:, SPLIT:]


def add_kernel(x_ref, y_ref, out_ref):
    scores = x_ref[:, :SPLIT].astype(F32) + y_ref[:, :SPLIT].astype(F32)
    out_ref[:, :SPLIT] = scores.astype(BF16)
    if out_ref.shape[1] > SPLIT:
        put_squares(out_ref, get_squares(x_ref, SPLIT) + get_squares(y_ref, SPLIT), SPLIT)


def factors(code, scale):
    high = scale.astype(BF16)
    low = (scale - high.astype(F32)).astype(BF16)
    number = lax.broadcasted_iota(jnp.int32, (PARENTS, BLOCK), 0)
    chosen = (number == code >> 6).astype(F32).astype(BF16)
    return jnp.dot(high, chosen, preferred_element_type=F32) + jnp.dot(
        low, chosen, preferred_element_type=F32
    )


def best(x, y, factor):
    return jnp.max((x.astype(F32) + y.astype(F32)) * factor, axis=0, keepdims=True) / (0.25 * D)


def finish_first_kernel(code_ref, x_ref, y_ref, totals_ref, factor_ref, centroids_ref, fit_ref):
    y, z, core = lax.axis_index("y"), lax.axis_index("z"), lax.axis_index("core")
    scale = lax.rsqrt((get_squares(x_ref, SPLIT) + get_squares(y_ref, SPLIT)) / D + EPS)
    lane = lax.broadcasted_iota(jnp.int32, (K, PARENTS), 1)
    own = jnp.sum(jnp.where(lane == y * 16 + z * 2 + core, scale, 0.0), axis=1, keepdims=True)
    centroids_ref[...] = (totals_ref[...] * own).astype(BF16)
    for start in range(0, SPLIT, BLOCK):
        part, later = slice(start, start + BLOCK), slice(SPLIT + start, SPLIT + start + BLOCK)
        fit_ref[:, part] = best(x_ref[:, part], y_ref[:, part], factors(code_ref[:, part], scale))
        factor_ref[:, part] = factors(code_ref[:, later], scale)


def finish_kernel(x_ref, y_ref, factor_ref, first_ref, fit_ref):
    fit_ref[:, :SPLIT] = first_ref[...]
    fit_ref[:, SPLIT:] = best(x_ref[...], y_ref[...], factor_ref[...])


def copy_kernel(x_ref, out_ref):
    out_ref[...] = x_ref[...]


def swap(x):
    return lax.ppermute(x, "core", [(0, 1), (1, 0)])


def left(x, axis):
    return lax.ppermute(x, axis, [(0, 1), (1, 0), (2, 3), (3, 2)])


def right(x, axis):
    return lax.ppermute(x, axis, [(0, 3), (3, 0), (1, 2), (2, 1)])


def turn(x, k):
    pairs = [(2 * i + core, 2 * (i ^ turned(k, core)) + core) for core in range(NC) for i in range(NY)]
    return lax.ppermute(x, ("y", "core"), pairs)


def body(embeddings, parent_ids, child_assignment):
    code = parent_ids.reshape(1, ROWS) * K + child_assignment.reshape(1, ROWS)
    code = call(copy_kernel, jax.ShapeDtypeStruct((1, ROWS), jnp.int32), [code], flops=LONG)
    own = (code, embeddings)
    other = tuple(swap(x) for x in own)

    def halves_of(dtype):
        return (jax.ShapeDtypeStruct((HALF, WIDTH), dtype),) * 2

    def sums(halves, dtype, groups, so_far=(), behind=(), flops=1000):
        return call(
            functools.partial(sums_kernel, halves, len(groups)),
            halves_of(dtype),
            [x for group in groups for x in group] + list(so_far),
            behind=behind,
            flops=flops,
        )

    halves = ((2, 0), (2, 1))
    far_low, far_high = sums(halves, BF16, [other], sums(halves, F32, [own]))
    got_low, got_high = left(far_low, "y"), right(far_high, "y")
    left_low, right_high = sums(((1, 0), (3, 1)), BF16, [own, other], behind=[far_low, far_high], flops=LONG)
    own_high, own_low = sums(((1, 1), (3, 0)), F32, [own, other], behind=[left_low, right_high])
    half = jax.ShapeDtypeStruct((HALF, WIDTH), BF16)
    right_low = call(hand_on_kernel, half, [own_low, got_low])
    left_high = call(hand_on_kernel, half, [own_high, got_high])
    kept = sums(((0, 0), (0, 1)), F32, [own, other], behind=[left_high, right_low])
    merged = call(
        merge_kernel,
        jax.ShapeDtypeStruct((PIECE, WIDTH), BF16),
        [*kept, left(left_low, "y"), right(right_low, "y"), left(left_high, "y"), right(right_high, "y")],
    )
    parts = lax.all_to_all(merged, "z", 0, 0, tiled=True)
    totals, copies = call(
        totals_kernel,
        (jax.ShapeDtypeStruct((K, WIDTH), F32), jax.ShapeDtypeStruct((PIECE, WIDTH), BF16)),
        [parts],
    )
    mine = lax.all_to_all(copies, "z", 0, 0, tiled=True)

    far = turn(mine, 2)
    near = [turn(mine, 1), turn(mine, 3)]

    plain = jax.ShapeDtypeStruct((K, ROWS), BF16)
    squared = jax.ShapeDtypeStruct((K, PARENTS), F32)
    state = call(
        functools.partial(scores_kernel, 2, (0,), True, True, False, (0, ROWS)),
        (plain, plain, squared),
        [*own, *other, mine],
    )
    state = call(
        functools.partial(scores_kernel, 2, (1, 3), False, True, False, (0, ROWS)),
        (plain, plain, squared),
        [*own, *other, *near, *state],
    )
    blocks = (2,)
    message = jax.ShapeDtypeStruct((K, SPLIT), BF16)
    long_message = jax.ShapeDtypeStruct((K, SPLIT + 2 * PARENTS), BF16)
    spans = ((0, SPLIT), (SPLIT, ROWS))
    (sent_a,) = call(
        functools.partial(scores_kernel, 1, blocks, False, True, True, spans[0]),
        (long_message,),
        [*other, far, *state[1:]],
    )
    (sent_b,) = call(
        functools.partial(scores_kernel, 1, blocks, False, False, False, spans[1]),
        (message,),
        [*other, far, state[1]],
        behind=[sent_a],
    )
    got_a, got_b = swap(sent_a), swap(sent_b)
    (kept_a,) = call(
        functools.partial(scores_kernel, 1, blocks, False, False, False, spans[0]),
        (message,),
        [*own, far, state[0]],
        behind=[sent_b],
    )
    a = call(join_kernel, long_message, [kept_a, sent_a, got_a])
    (kept_b,) = call(
        functools.partial(scores_kernel, 1, blocks, False, False, False, spans[1]),
        (message,),
        [*own, far, state[0]],
        behind=[a],
    )
    b = call(join_kernel, message, [kept_b, sent_b, got_b])

    a = call(add_kernel, long_message, [a, left(a, "feat")])
    b = call(add_kernel, message, [b, right(b, "feat")])
    factor, centroids, first = call(
        finish_first_kernel,
        (
            jax.ShapeDtypeStruct((K, SPLIT), F32),
            jax.ShapeDtypeStruct((K, WIDTH), BF16),
            jax.ShapeDtypeStruct((1, SPLIT), F32),
        ),
        [code, a, right(a, "feat"), totals],
    )
    fit = call(
        finish_kernel, jax.ShapeDtypeStruct((1, ROWS), F32), [b, left(b, "feat"), factor, first]
    )
    return centroids, fit.reshape(ROWS)


def solution(mesh):
    split = Mesh(mesh.devices.reshape(NY, NZ, NC, NX), ("y", "z", "core", "feat"))
    rows = ("y", "z", "core")
    in_specs = (P(rows, "feat"), P(rows, None), P(rows))
    out_specs = (P(rows, "feat"), P(rows))
    return jax.shard_map(body, mesh=split, in_specs=in_specs, out_specs=out_specs, check_vma=False)
```

```python
import functools

import jax
import jax.numpy as jnp
from jax import lax
from jax.experimental import pallas as pl
from jax.experimental.pallas import tpu as pltpu
from jax.sharding import Mesh, PartitionSpec as P

D = 1024
K = 64
EPS = 1e-06
NY, NZ, NC, NX = 4, 8, 2, 4
PARENTS = NY * NZ * NC
ROWS = 2048
WIDTH = 256
PIECE = NZ * K
HALF = PIECE // 2
SPLIT = ROWS // 2
BLOCK = 512
VMEM = 24 * 1024 * 1024
LONG = 1 << 32

F32 = jnp.float32
BF16 = jnp.bfloat16


def call(kernel, out_shape, operands, behind=(), flops=1000):
    vmem = pl.BlockSpec(memory_space=pltpu.VMEM)
    count = len(operands)

    def skipping(*refs):
        kernel(*refs[:count], *refs[count + len(behind) :])

    return pl.pallas_call(
        skipping,
        out_shape=out_shape,
        in_specs=[vmem] * (count + len(behind)),
        out_specs=jax.tree.map(lambda _: vmem, out_shape),
        compiler_params=pltpu.CompilerParams(vmem_limit_bytes=VMEM),
        cost_estimate=pl.CostEstimate(flops=flops, bytes_accessed=1000, transcendentals=0),
    )(*operands, *behind)


def add_members(totals, halves, codes, rows, start):
    y, core = lax.axis_index("y"), lax.axis_index("core")
    span = slice(start, start + BLOCK)
    code = codes[:, span]
    parent = code >> 6
    block = rows[span, :]
    child = lax.broadcasted_iota(jnp.int32, (HALF, BLOCK), 0)
    for number, (k, upper) in enumerate(halves):
        inside = ((parent >> 4) == (y ^ k)) & ((parent & 1) == core)
        local = jnp.where(inside, ((parent >> 1) & 7) * K + (code & (K - 1)) - upper * HALF, -1)
        member = (child == local).astype(F32).astype(BF16)
        totals[number] += jnp.dot(member, block, preferred_element_type=F32)


def sums_kernel(halves, groups, *refs):
    outs, so_far = refs[-len(halves) :], refs[2 * groups : -len(halves)]
    totals = [x[...].astype(F32) for x in so_far] or [jnp.zeros((HALF, WIDTH), F32) for _ in halves]
    for group in range(groups):
        for start in range(0, ROWS, BLOCK):
            add_members(totals, halves, *refs[2 * group : 2 * group + 2], start)
    for out, total in zip(outs, totals):
        out[...] = total.astype(out.dtype)


def hand_on_kernel(own_ref, got_ref, out_ref):
    out_ref[...] = (own_ref[...] + got_ref[...].astype(F32)).astype(BF16)


def merge_kernel(low_ref, high_ref, low_a, low_b, high_a, high_b, out_ref):
    out_ref[:HALF, :] = (low_ref[...] + low_a[...].astype(F32) + low_b[...].astype(F32)).astype(BF16)
    out_ref[HALF:, :] = (high_ref[...] + high_a[...].astype(F32) + high_b[...].astype(F32)).astype(BF16)


def totals_kernel(parts_ref, totals_ref, copies_ref):
    total = parts_ref[0:K, :].astype(F32)
    for z in range(1, NZ):
        total += parts_ref[z * K : (z + 1) * K, :].astype(F32)
    totals_ref[...] = total
    rounded = total.astype(BF16)
    for z in range(NZ):
        copies_ref[z * K : (z + 1) * K, :] = rounded


def scores_kernel(groups, blocks, first, with_squares, packed, span, *refs):
    y, core = lax.axis_index("y"), lax.axis_index("core")
    group_refs, refs = refs[: 2 * groups], refs[2 * groups :]
    block_refs, refs = refs[: len(blocks)], refs[len(blocks) :]
    numbers = [(y ^ k) * 16 + core for k in blocks]
    scores_in = squares_in = None
    if not first:
        scores_in, refs = refs[:groups], refs[groups:]
        if with_squares:
            squares_in, refs = refs[0], refs[1:]
    if with_squares:
        lane = lax.broadcasted_iota(jnp.int32, (K, PARENTS), 1)
        squares = jnp.zeros((K, PARENTS), F32) if first else squares_in[...]
        for number, block_ref in zip(numbers, block_refs):
            for z in range(NZ):
                block = block_ref[z * K : (z + 1) * K, :].astype(F32)
                square = jnp.sum(block * block, axis=1, keepdims=True)
                squares = jnp.where(lane == number + 2 * z, square, squares)
        if packed:
            put_squares(refs[0], squares, SPLIT)
        else:
            refs[groups][...] = squares
    for group in range(groups):
        codes, rows_ref = group_refs[2 * group : 2 * group + 2]
        for start in range(*span, BLOCK):
            part = slice(start, start + BLOCK)
            rows, parent = rows_ref[part, :], codes[:, part] >> 6
            chosen = jnp.zeros((K, BLOCK), F32) if first else scores_in[group][:, part].astype(F32)
            for number, block_ref in zip(numbers, block_refs):
                product = lax.dot_general(
                    block_ref[...], rows, (((1,), (1,)), ((), ())), preferred_element_type=F32
                )
                for z in range(NZ):
                    chosen = jnp.where(parent == number + 2 * z, product[z * K : (z + 1) * K, :], chosen)
            refs[group][:, start - span[0] : start - span[0] + BLOCK] = chosen.astype(BF16)


def put_squares(out_ref, squares, at):
    high = squares.astype(BF16)
    out_ref[:, at : at + PARENTS] = high
    out_ref[:, at + PARENTS : at + 2 * PARENTS] = (squares - high.astype(F32)).astype(BF16)


def get_squares(ref, at):
    return ref[:, at : at + PARENTS].astype(F32) + ref[:, at + PARENTS : at + 2 * PARENTS].astype(F32)


def join_kernel(own_ref, sent_ref, arrived_ref, out_ref):
    out_ref[:, :SPLIT] = own_ref[...] + arrived_ref[:, :SPLIT]
    if out_ref.shape[1] > SPLIT:
        out_ref[:, SPLIT:] = sent_ref[:, SPLIT:] + arrived_ref[:, SPLIT:]


def add_kernel(x_ref, y_ref, out_ref):
    scores = x_ref[:, :SPLIT].astype(F32) + y_ref[:, :SPLIT].astype(F32)
    out_ref[:, :SPLIT] = scores.astype(BF16)
    if out_ref.shape[1] > SPLIT:
        put_squares(out_ref, get_squares(x_ref, SPLIT) + get_squares(y_ref, SPLIT), SPLIT)


def factors(code, scale):
    high = scale.astype(BF16)
    low = (scale - high.astype(F32)).astype(BF16)
    number = lax.broadcasted_iota(jnp.int32, (PARENTS, BLOCK), 0)
    chosen = (number == code >> 6).astype(F32).astype(BF16)
    return jnp.dot(high, chosen, preferred_element_type=F32) + jnp.dot(
        low, chosen, preferred_element_type=F32
    )


def best(x, y, factor):
    return jnp.max((x.astype(F32) + y.astype(F32)) * factor, axis=0, keepdims=True) / (0.25 * D)


def finish_first_kernel(code_ref, x_ref, y_ref, totals_ref, factor_ref, centroids_ref, fit_ref):
    y, z, core = lax.axis_index("y"), lax.axis_index("z"), lax.axis_index("core")
    scale = lax.rsqrt((get_squares(x_ref, SPLIT) + get_squares(y_ref, SPLIT)) / D + EPS)
    lane = lax.broadcasted_iota(jnp.int32, (K, PARENTS), 1)
    own = jnp.sum(jnp.where(lane == y * 16 + z * 2 + core, scale, 0.0), axis=1, keepdims=True)
    centroids_ref[...] = (totals_ref[...] * own).astype(BF16)
    for start in range(0, SPLIT, BLOCK):
        part, later = slice(start, start + BLOCK), slice(SPLIT + start, SPLIT + start + BLOCK)
        fit_ref[:, part] = best(x_ref[:, part], y_ref[:, part], factors(code_ref[:, part], scale))
        factor_ref[:, part] = factors(code_ref[:, later], scale)


def finish_kernel(x_ref, y_ref, factor_ref, first_ref, fit_ref):
    fit_ref[:, :SPLIT] = first_ref[...]
    fit_ref[:, SPLIT:] = best(x_ref[...], y_ref[...], factor_ref[...])


def copy_kernel(x_ref, out_ref):
    out_ref[...] = x_ref[...]


def swap(x):
    return lax.ppermute(x, "core", [(0, 1), (1, 0)])


def left(x, axis):
    return lax.ppermute(x, axis, [(0, 1), (1, 0), (2, 3), (3, 2)])


def right(x, axis):
    return lax.ppermute(x, axis, [(0, 3), (3, 0), (1, 2), (2, 1)])


def across(x):
    return lax.ppermute(x, "y", [(i, i ^ 2) for i in range(NY)])


def body(embeddings, parent_ids, child_assignment):
    code = parent_ids.reshape(1, ROWS) * K + child_assignment.reshape(1, ROWS)
    code = call(copy_kernel, jax.ShapeDtypeStruct((1, ROWS), jnp.int32), [code], flops=LONG)
    own = (code, embeddings)
    other = tuple(swap(x) for x in own)

    def halves_of(dtype):
        return (jax.ShapeDtypeStruct((HALF, WIDTH), dtype),) * 2

    def sums(halves, dtype, groups, so_far=(), behind=(), flops=1000):
        return call(
            functools.partial(sums_kernel, halves, len(groups)),
            halves_of(dtype),
            [x for group in groups for x in group] + list(so_far),
            behind=behind,
            flops=flops,
        )

    halves = ((2, 0), (2, 1))
    far_low, far_high = sums(halves, BF16, [other], sums(halves, F32, [own]))
    got_low, got_high = left(far_low, "y"), right(far_high, "y")
    left_low, right_high = sums(((1, 0), (3, 1)), BF16, [own, other], behind=[far_low, far_high], flops=LONG)
    own_high, own_low = sums(((1, 1), (3, 0)), F32, [own, other], behind=[left_low, right_high])
    half = jax.ShapeDtypeStruct((HALF, WIDTH), BF16)
    right_low = call(hand_on_kernel, half, [own_low, got_low])
    left_high = call(hand_on_kernel, half, [own_high, got_high])
    kept = sums(((0, 0), (0, 1)), F32, [own, other], behind=[left_high, right_low])
    merged = call(
        merge_kernel,
        jax.ShapeDtypeStruct((PIECE, WIDTH), BF16),
        [*kept, left(left_low, "y"), right(right_low, "y"), left(left_high, "y"), right(right_high, "y")],
    )
    parts = lax.all_to_all(merged, "z", 0, 0, tiled=True)
    totals, copies = call(
        totals_kernel,
        (jax.ShapeDtypeStruct((K, WIDTH), F32), jax.ShapeDtypeStruct((PIECE, WIDTH), BF16)),
        [parts],
    )
    mine = lax.all_to_all(copies, "z", 0, 0, tiled=True)

    far = across(mine)
    near = [left(mine, "y"), right(mine, "y")]

    plain = jax.ShapeDtypeStruct((K, ROWS), BF16)
    squared = jax.ShapeDtypeStruct((K, PARENTS), F32)
    state = call(
        functools.partial(scores_kernel, 2, (0,), True, True, False, (0, ROWS)),
        (plain, plain, squared),
        [*own, *other, mine],
    )
    state = call(
        functools.partial(scores_kernel, 2, (1, 3), False, True, False, (0, ROWS)),
        (plain, plain, squared),
        [*own, *other, *near, *state],
    )
    blocks = (2,)
    message = jax.ShapeDtypeStruct((K, SPLIT), BF16)
    long_message = jax.ShapeDtypeStruct((K, SPLIT + 2 * PARENTS), BF16)
    spans = ((0, SPLIT), (SPLIT, ROWS))
    (sent_a,) = call(
        functools.partial(scores_kernel, 1, blocks, False, True, True, spans[0]),
        (long_message,),
        [*other, far, *state[1:]],
    )
    (sent_b,) = call(
        functools.partial(scores_kernel, 1, blocks, False, False, False, spans[1]),
        (message,),
        [*other, far, state[1]],
        behind=[sent_a],
    )
    got_a, got_b = swap(sent_a), swap(sent_b)
    (kept_a,) = call(
        functools.partial(scores_kernel, 1, blocks, False, False, False, spans[0]),
        (message,),
        [*own, far, state[0]],
        behind=[sent_b],
    )
    a = call(join_kernel, long_message, [kept_a, sent_a, got_a])
    (kept_b,) = call(
        functools.partial(scores_kernel, 1, blocks, False, False, False, spans[1]),
        (message,),
        [*own, far, state[0]],
        behind=[a],
    )
    b = call(join_kernel, message, [kept_b, sent_b, got_b])

    a = call(add_kernel, long_message, [a, left(a, "feat")])
    b = call(add_kernel, message, [b, right(b, "feat")])
    factor, centroids, first = call(
        finish_first_kernel,
        (
            jax.ShapeDtypeStruct((K, SPLIT), F32),
            jax.ShapeDtypeStruct((K, WIDTH), BF16),
            jax.ShapeDtypeStruct((1, SPLIT), F32),
        ),
        [code, a, right(a, "feat"), totals],
    )
    fit = call(
        finish_kernel, jax.ShapeDtypeStruct((1, ROWS), F32), [b, left(b, "feat"), factor, first]
    )
    return centroids, fit.reshape(ROWS)


def solution(mesh):
    split = Mesh(mesh.devices.reshape(NY, NZ, NC, NX), ("y", "z", "core", "feat"))
    rows = ("y", "z", "core")
    in_specs = (P(rows, "feat"), P(rows, None), P(rows))
    out_specs = (P(rows, "feat"), P(rows))
    return jax.shard_map(body, mesh=split, in_specs=in_specs, out_specs=out_specs, check_vma=False)
```

```python
import functools

import jax
import jax.numpy as jnp
from jax import lax
from jax.experimental import pallas as pl
from jax.experimental.pallas import tpu as pltpu
from jax.sharding import Mesh, PartitionSpec as P

D = 1024
K = 64
EPS = 1e-06
NY, NZ, NC, NX = 4, 8, 2, 4
PARENTS = NY * NZ * NC
ROWS = 2048
WIDTH = 256
PIECE = NZ * K
HALF = PIECE // 2
SPLIT = ROWS // 2
BLOCK = 512
VMEM = 24 * 1024 * 1024
LONG = 1 << 32

F32 = jnp.float32
BF16 = jnp.bfloat16


def call(kernel, out_shape, operands, behind=(), flops=1000):
    vmem = pl.BlockSpec(memory_space=pltpu.VMEM)
    count = len(operands)

    def skipping(*refs):
        kernel(*refs[:count], *refs[count + len(behind) :])

    return pl.pallas_call(
        skipping,
        out_shape=out_shape,
        in_specs=[vmem] * (count + len(behind)),
        out_specs=jax.tree.map(lambda _: vmem, out_shape),
        compiler_params=pltpu.CompilerParams(vmem_limit_bytes=VMEM),
        cost_estimate=pl.CostEstimate(flops=flops, bytes_accessed=1000, transcendentals=0),
    )(*operands, *behind)


def add_members(totals, halves, codes, rows, start):
    y, core = lax.axis_index("y"), lax.axis_index("core")
    span = slice(start, start + BLOCK)
    code = codes[:, span]
    parent = code >> 6
    block = rows[span, :]
    child = lax.broadcasted_iota(jnp.int32, (HALF, BLOCK), 0)
    for number, (k, upper) in enumerate(halves):
        inside = ((parent >> 4) == (y ^ k)) & ((parent & 1) == core)
        local = jnp.where(inside, ((parent >> 1) & 7) * K + (code & (K - 1)) - upper * HALF, -1)
        member = (child == local).astype(F32).astype(BF16)
        totals[number] += jnp.dot(member, block, preferred_element_type=F32)


def sums_kernel(halves, groups, *refs):
    outs, so_far = refs[-len(halves) :], refs[2 * groups : -len(halves)]
    totals = [x[...].astype(F32) for x in so_far] or [jnp.zeros((HALF, WIDTH), F32) for _ in halves]
    for group in range(groups):
        for start in range(0, ROWS, BLOCK):
            add_members(totals, halves, *refs[2 * group : 2 * group + 2], start)
    for out, total in zip(outs, totals):
        out[...] = total.astype(out.dtype)


def hand_on_kernel(own_ref, got_ref, out_ref):
    out_ref[...] = (own_ref[...] + got_ref[...].astype(F32)).astype(BF16)


def merge_kernel(low_ref, high_ref, low_a, low_b, high_a, high_b, out_ref):
    out_ref[:HALF, :] = (low_ref[...] + low_a[...].astype(F32) + low_b[...].astype(F32)).astype(BF16)
    out_ref[HALF:, :] = (high_ref[...] + high_a[...].astype(F32) + high_b[...].astype(F32)).astype(BF16)


def totals_kernel(parts_ref, totals_ref, copies_ref):
    total = parts_ref[0:K, :].astype(F32)
    for z in range(1, NZ):
        total += parts_ref[z * K : (z + 1) * K, :].astype(F32)
    totals_ref[...] = total
    rounded = total.astype(BF16)
    for z in range(NZ):
        copies_ref[z * K : (z + 1) * K, :] = rounded


def scores_kernel(groups, blocks, first, with_squares, packed, span, *refs):
    y, core = lax.axis_index("y"), lax.axis_index("core")
    group_refs, refs = refs[: 2 * groups], refs[2 * groups :]
    block_refs, refs = refs[: len(blocks)], refs[len(blocks) :]
    numbers = [(y ^ k) * 16 + core for k in blocks]
    scores_in = squares_in = None
    if not first:
        scores_in, refs = refs[:groups], refs[groups:]
        if with_squares:
            squares_in, refs = refs[0], refs[1:]
    if with_squares:
        lane = lax.broadcasted_iota(jnp.int32, (K, PARENTS), 1)
        squares = jnp.zeros((K, PARENTS), F32) if first else squares_in[...]
        for number, block_ref in zip(numbers, block_refs):
            for z in range(NZ):
                block = block_ref[z * K : (z + 1) * K, :].astype(F32)
                square = jnp.sum(block * block, axis=1, keepdims=True)
                squares = jnp.where(lane == number + 2 * z, square, squares)
        if packed:
            put_squares(refs[0], squares, SPLIT)
        else:
            refs[groups][...] = squares
    for group in range(groups):
        codes, rows_ref = group_refs[2 * group : 2 * group + 2]
        for start in range(*span, BLOCK):
            part = slice(start, start + BLOCK)
            rows, parent = rows_ref[part, :], codes[:, part] >> 6
            chosen = jnp.zeros((K, BLOCK), F32) if first else scores_in[group][:, part].astype(F32)
            for number, block_ref in zip(numbers, block_refs):
                product = lax.dot_general(
                    block_ref[...], rows, (((1,), (1,)), ((), ())), preferred_element_type=F32
                )
                for z in range(NZ):
                    chosen = jnp.where(parent == number + 2 * z, product[z * K : (z + 1) * K, :], chosen)
            refs[group][:, start - span[0] : start - span[0] + BLOCK] = chosen.astype(BF16)


def put_squares(out_ref, squares, at):
    high = squares.astype(BF16)
    out_ref[:, at : at + PARENTS] = high
    out_ref[:, at + PARENTS : at + 2 * PARENTS] = (squares - high.astype(F32)).astype(BF16)


def get_squares(ref, at):
    return ref[:, at : at + PARENTS].astype(F32) + ref[:, at + PARENTS : at + 2 * PARENTS].astype(F32)


def join_kernel(own_ref, sent_ref, arrived_ref, out_ref):
    out_ref[:, :SPLIT] = own_ref[...] + arrived_ref[:, :SPLIT]
    if out_ref.shape[1] > SPLIT:
        out_ref[:, SPLIT:] = sent_ref[:, SPLIT:] + arrived_ref[:, SPLIT:]


def add_kernel(x_ref, y_ref, out_ref):
    scores = x_ref[:, :SPLIT].astype(F32) + y_ref[:, :SPLIT].astype(F32)
    out_ref[:, :SPLIT] = scores.astype(BF16)
    if out_ref.shape[1] > SPLIT:
        put_squares(out_ref, get_squares(x_ref, SPLIT) + get_squares(y_ref, SPLIT), SPLIT)


def factors(code, scale):
    high = scale.astype(BF16)
    low = (scale - high.astype(F32)).astype(BF16)
    number = lax.broadcasted_iota(jnp.int32, (PARENTS, BLOCK), 0)
    chosen = (number == code >> 6).astype(F32).astype(BF16)
    return jnp.dot(high, chosen, preferred_element_type=F32) + jnp.dot(
        low, chosen, preferred_element_type=F32
    )


def best(x, y, factor):
    return jnp.max((x.astype(F32) + y.astype(F32)) * factor, axis=0, keepdims=True) / (0.25 * D)


def finish_first_kernel(code_ref, x_ref, y_ref, totals_ref, factor_ref, centroids_ref, fit_ref):
    y, z, core = lax.axis_index("y"), lax.axis_index("z"), lax.axis_index("core")
    scale = lax.rsqrt((get_squares(x_ref, SPLIT) + get_squares(y_ref, SPLIT)) / D + EPS)
    lane = lax.broadcasted_iota(jnp.int32, (K, PARENTS), 1)
    own = jnp.sum(jnp.where(lane == y * 16 + z * 2 + core, scale, 0.0), axis=1, keepdims=True)
    centroids_ref[...] = (totals_ref[...] * own).astype(BF16)
    for start in range(0, SPLIT, BLOCK):
        part, later = slice(start, start + BLOCK), slice(SPLIT + start, SPLIT + start + BLOCK)
        fit_ref[:, part] = best(x_ref[:, part], y_ref[:, part], factors(code_ref[:, part], scale))
        factor_ref[:, part] = factors(code_ref[:, later], scale)


def finish_kernel(x_ref, y_ref, factor_ref, first_ref, fit_ref):
    fit_ref[:, :SPLIT] = first_ref[...]
    fit_ref[:, SPLIT:] = best(x_ref[...], y_ref[...], factor_ref[...])


def copy_kernel(x_ref, out_ref):
    out_ref[...] = x_ref[...]


def swap(x):
    return lax.ppermute(x, "core", [(0, 1), (1, 0)])


def left(x, axis):
    return lax.ppermute(x, axis, [(0, 1), (1, 0), (2, 3), (3, 2)])


def right(x, axis):
    return lax.ppermute(x, axis, [(0, 3), (3, 0), (1, 2), (2, 1)])


def across(x):
    return lax.ppermute(x, "y", [(i, i ^ 2) for i in range(NY)])


def body(embeddings, parent_ids, child_assignment):
    code = parent_ids.reshape(1, ROWS) * K + child_assignment.reshape(1, ROWS)
    code = call(copy_kernel, jax.ShapeDtypeStruct((1, ROWS), jnp.int32), [code], flops=LONG)
    own = (code, embeddings)
    other = tuple(swap(x) for x in own)

    def halves_of(dtype):
        return (jax.ShapeDtypeStruct((HALF, WIDTH), dtype),) * 2

    def sums(halves, dtype, groups, so_far=(), behind=(), flops=1000):
        return call(
            functools.partial(sums_kernel, halves, len(groups)),
            halves_of(dtype),
            [x for group in groups for x in group] + list(so_far),
            behind=behind,
            flops=flops,
        )

    halves = ((2, 0), (2, 1))
    far_low, far_high = sums(halves, BF16, [other], sums(halves, F32, [own]))
    got_low, got_high = right(far_low, "y"), left(far_high, "y")
    right_low, left_high = sums(((3, 0), (1, 1)), BF16, [own, other], behind=[far_low, far_high], flops=LONG)
    own_high, own_low = sums(((3, 1), (1, 0)), F32, [own, other], behind=[right_low, left_high])
    half = jax.ShapeDtypeStruct((HALF, WIDTH), BF16)
    left_low = call(hand_on_kernel, half, [own_low, got_low])
    right_high = call(hand_on_kernel, half, [own_high, got_high])
    kept = sums(((0, 0), (0, 1)), F32, [own, other], behind=[right_high, left_low])
    merged = call(
        merge_kernel,
        jax.ShapeDtypeStruct((PIECE, WIDTH), BF16),
        [*kept, right(right_low, "y"), left(left_low, "y"), right(right_high, "y"), left(left_high, "y")],
    )
    parts = lax.all_to_all(merged, "z", 0, 0, tiled=True)
    totals, copies = call(
        totals_kernel,
        (jax.ShapeDtypeStruct((K, WIDTH), F32), jax.ShapeDtypeStruct((PIECE, WIDTH), BF16)),
        [parts],
    )
    mine = lax.all_to_all(copies, "z", 0, 0, tiled=True)

    far = across(mine)
    near = [left(mine, "y"), right(mine, "y")]

    plain = jax.ShapeDtypeStruct((K, ROWS), BF16)
    squared = jax.ShapeDtypeStruct((K, PARENTS), F32)
    state = call(
        functools.partial(scores_kernel, 2, (0,), True, True, False, (0, ROWS)),
        (plain, plain, squared),
        [*own, *other, mine],
    )
    state = call(
        functools.partial(scores_kernel, 2, (1, 3), False, True, False, (0, ROWS)),
        (plain, plain, squared),
        [*own, *other, *near, *state],
    )
    blocks = (2,)
    message = jax.ShapeDtypeStruct((K, SPLIT), BF16)
    long_message = jax.ShapeDtypeStruct((K, SPLIT + 2 * PARENTS), BF16)
    spans = ((0, SPLIT), (SPLIT, ROWS))
    (sent_a,) = call(
        functools.partial(scores_kernel, 1, blocks, False, True, True, spans[0]),
        (long_message,),
        [*other, far, *state[1:]],
    )
    (sent_b,) = call(
        functools.partial(scores_kernel, 1, blocks, False, False, False, spans[1]),
        (message,),
        [*other, far, state[1]],
        behind=[sent_a],
    )
    got_a, got_b = swap(sent_a), swap(sent_b)
    (kept_a,) = call(
        functools.partial(scores_kernel, 1, blocks, False, False, False, spans[0]),
        (message,),
        [*own, far, state[0]],
        behind=[sent_b],
    )
    a = call(join_kernel, long_message, [kept_a, sent_a, got_a])
    (kept_b,) = call(
        functools.partial(scores_kernel, 1, blocks, False, False, False, spans[1]),
        (message,),
        [*own, far, state[0]],
        behind=[a],
    )
    b = call(join_kernel, message, [kept_b, sent_b, got_b])

    a = call(add_kernel, long_message, [a, left(a, "feat")])
    b = call(add_kernel, message, [b, right(b, "feat")])
    factor, centroids, first = call(
        finish_first_kernel,
        (
            jax.ShapeDtypeStruct((K, SPLIT), F32),
            jax.ShapeDtypeStruct((K, WIDTH), BF16),
            jax.ShapeDtypeStruct((1, SPLIT), F32),
        ),
        [code, a, right(a, "feat"), totals],
    )
    fit = call(
        finish_kernel, jax.ShapeDtypeStruct((1, ROWS), F32), [b, left(b, "feat"), factor, first]
    )
    return centroids, fit.reshape(ROWS)


def solution(mesh):
    split = Mesh(mesh.devices.reshape(NY, NZ, NC, NX), ("y", "z", "core", "feat"))
    rows = ("y", "z", "core")
    in_specs = (P(rows, "feat"), P(rows, None), P(rows))
    out_specs = (P(rows, "feat"), P(rows))
    return jax.shard_map(body, mesh=split, in_specs=in_specs, out_specs=out_specs, check_vma=False)
```
